32 devices in a mesh: groups: 2 (over y), ctx: 16 (over z, x, core).
Axes of the slice: x: 2, y: 2, z: 4, core: 2. Of those that a mesh axis runs over, the one named last changes fastest.
Arguments:
- inputs: bfloat16 [4096, 1536], P(('groups', 'ctx')), parts along dimension 0, may hold values from -6 to 6
- cotangent: bfloat16 [4096, 1536], P(('groups', 'ctx')), parts along dimension 0, may hold values from -6 to 6
- w_taps: bfloat16 [4608, 384], replicated, may hold values from -0.09375 to 0.09375
- w_out: bfloat16 [384, 1536], replicated, may hold values from -0.3125 to 0.3125
Outputs:
- outputs: bfloat16 [4096, 1536], P(('groups', 'ctx')), parts along dimension 0
- grad_input: bfloat16 [4096, 1536], P(('groups', 'ctx')), parts along dimension 0
- grad_taps: float32 [9216, 384], P(('groups', 'ctx')), parts along dimension 0
The draws below stay inside these ranges and needn't reach their ends.
There are 2 independent parts, one for each index of `groups`. The reference program is written for one: setup_inputs(seed, part) draws one part's arguments, and reference() takes and returns one part's arrays. A program takes and returns all parts, laid end to end along the dimension named above; an argument that names none is the same for every part. Nothing has to cross between parts.
All inputs are finite; a program needn't handle non-finite values.
Results may differ from the reference program's by a relative error of at most 0.0053.
Values may be sent and summed in bfloat16 or wider, within the bound.
A program may use at most 64 MiB of HBM per device.

```python
import math
import jax
import jax.numpy as jnp
from jax import lax

TRUNK_CHANNELS = 1536
M = 384
BINS = 2048
DILATION_STEP = 256


def raised(result, stream_key, source, target, shards_of, factor):
    def block_of(dim):
        return (jnp.arange(result.shape[dim]) // (result.shape[dim] // shards_of)).reshape((-1,) + (1,) * (result.ndim - 1 - dim))

    first = jax.random.permutation(stream_key, shards_of)[block_of(target)]
    far = (block_of(target) + shards_of // 2) % shards_of
    return jnp.where((block_of(source) == first) | (block_of(source) == far), factor * result, result)


def shard_levels(key, extent, shards, low, largest):
    def one(dim, shards_of):
        heights = jax.random.uniform(jax.random.fold_in(jax.random.fold_in(key, 6), dim), (shards_of,), jnp.float32, low / len(shards), largest / len(shards))
        return jnp.repeat(jnp.exp(heights), extent[dim] // shards_of).reshape((-1,) + (1,) * (len(extent) - dim - 1))

    factor_of = one(*shards[0])
    for cut in shards[1:]:
        factor_of = factor_of * one(*cut)
    return factor_of


def bell_draw(key, dims, width, most, split=(), dtype=jnp.bfloat16):
    entries = jax.random.normal(key, dims, jnp.float32) * width
    if len(split) > 0:
        entries = shard_levels(key, dims, split, -0.22, 0.18) * entries
    return jnp.clip(entries, min=-most, max=most).astype(dtype)


def bell_draw_with(key, dims, width, limit, pieces, heavy, kind=jnp.bfloat16):
    array = width * jax.random.normal(key, dims, jnp.float32)
    if pieces:
        array = array * shard_levels(key, dims, pieces, -0.22, 0.18)
    return jnp.clip(raised(array, jax.random.fold_in(key, 3), *heavy), -limit, limit).astype(kind)


def setup_inputs(seed: int = 0, part: int = 0) -> dict:
    keys = jax.random.split(jax.random.key(seed), 5)
    part_keys = jax.random.split(jax.random.fold_in(keys[4], part), 5)
    return {
        "inputs": bell_draw(part_keys[0], (BINS, TRUNK_CHANNELS), 1.0, 6.0, ((0, 16),)),
        "cotangent": bell_draw_with(part_keys[1], (BINS, TRUNK_CHANNELS), 1.0, 6.0, ((0, 16),), (0, 1, 16, 2.0)),
        "w_taps": bell_draw(keys[2], (3 * TRUNK_CHANNELS, M), (3 * TRUNK_CHANNELS) ** -0.5, 0.09375),
        "w_out": bell_draw(keys[3], (M, TRUNK_CHANNELS), M ** -0.5, 0.3125),
    }


def normalize(values):
    centre = lax.optimization_barrier(jnp.mean(values, axis=1, keepdims=True))
    spread = lax.optimization_barrier(jnp.mean(jnp.square(values - centre), axis=1, keepdims=True))
    return jax.nn.gelu((values - centre) * lax.rsqrt(spread + 1e-05))

def preceding_bins(field, dist):
    return jnp.pad(field, ((dist, 0), (0, 0)))[:field.shape[0]]

def following_bins(field, dist):
    return jnp.pad(field, ((0, dist), (0, 0)))[dist:]

def reference(inputs, cotangent, w_taps, w_out):
    as_float = inputs.astype(jnp.float32)
    acts_full, act_vjp = jax.vjp(normalize, as_float)
    activation_rows = acts_full.astype(jnp.bfloat16)
    stacked_taps_input = jnp.concatenate([preceding_bins(activation_rows, DILATION_STEP), activation_rows, following_bins(activation_rows, DILATION_STEP)], axis=1)
    hidden = jnp.dot(stacked_taps_input, w_taps, preferred_element_type=jnp.float32)
    gated_full, gelu_vjp = jax.vjp(jax.nn.gelu, hidden)
    gated = gated_full.astype(jnp.bfloat16)
    outputs = (as_float + jnp.dot(gated, w_out, preferred_element_type=jnp.float32)).astype(jnp.bfloat16)
    back = lax.dot_general(cotangent, w_out, (((1,), (1,)), ((), ())), preferred_element_type=jnp.float32)
    dhid = gelu_vjp(back)[0].astype(jnp.bfloat16)
    grad_scale = 1.0 / math.sqrt(BINS)
    grad_taps = lax.dot_general(stacked_taps_input, dhid, (((0,), (0,)), ((), ())), preferred_element_type=jnp.float32) * grad_scale
    tap_products = lax.dot_general(dhid, w_taps, (((1,), (1,)), ((), ())), preferred_element_type=jnp.float32)
    activation_gradient = following_bins(tap_products[:, :TRUNK_CHANNELS], DILATION_STEP) + tap_products[:, TRUNK_CHANNELS:2 * TRUNK_CHANNELS] + preceding_bins(tap_products[:, 2 * TRUNK_CHANNELS:], DILATION_STEP)
    grad_input = (cotangent.astype(jnp.float32) + act_vjp(activation_gradient)[0]).astype(jnp.bfloat16)
    return (outputs, grad_input, grad_taps)
```

```python
import functools
import math

import jax
import jax.numpy as jnp
from jax import lax
from jax.experimental import pallas as pl
from jax.experimental.pallas import tpu as pltpu
from jax.sharding import PartitionSpec as P

F32 = jnp.float32
BF16 = jnp.bfloat16
C0 = math.sqrt(2.0 / math.pi)
C1 = 0.044715
CHUNK = 16
SUB = 96


def nt_dot(a, b):
    return lax.dot_general(a, b, (((1,), (1,)), ((), ())), preferred_element_type=F32)


def gelu_pair(v):
    sq = v * v
    t = jnp.tanh(v * (C0 + (C0 * C1) * sq))
    half = 0.5 + 0.5 * t
    value = v * half
    slope = half + (0.5 * v) * (1.0 - t * t) * (C0 + (3.0 * C0 * C1) * sq)
    return value, slope


def fused(
    scale, x_ref, ct_ref, wt_hbm, wo_hbm, out_ref, gi_ref, gt_ref,
    wt, wo, acts, acts_t, v_buf, slope_buf, r_buf, blocks, dh, h_send, h_recv, p_send, p_recv,
    w_sem, hs_sem, hr_sem, as_sem, ar_sem, ds_sem, dr_sem, es_sem, ps_sem, pr_sem,
):
    me = lax.axis_index("ctx")
    rows, channels = x_ref.shape
    own_rows = gt_ref.shape[0]
    half = me // 8
    base = half * 8
    place = me - base
    core = me % 2
    pair = place // 2
    mirror = (me + 8) % 16

    def to(index):
        return {"ctx": index}

    def remote(src, dst, send, recv, index):
        return pltpu.make_async_remote_copy(
            src_ref=src, dst_ref=dst, send_sem=send, recv_sem=recv,
            device_id=to(index), device_id_type=pl.DeviceIdType.MESH,
        )

    w_copies = [
        pltpu.make_async_copy(wt_hbm.at[pl.ds(k * channels, channels)],
                              wt.at[pl.ds(k * channels, channels)], w_sem.at[n])
        for n, k in enumerate((0, 2, 1))
    ]
    w_copies.append(pltpu.make_async_copy(wo_hbm, wo, w_sem.at[3]))
    for copy in w_copies:
        copy.start()

    barrier = pltpu.get_barrier_semaphore()
    for i in range(1, 16):
        pl.semaphore_signal(barrier, inc=1, device_id=to((me + i) % 16),
                            device_id_type=pl.DeviceIdType.MESH)

    for n in range(rows // CHUNK):
        part = pl.ds(n * CHUNK, CHUNK)
        x = x_ref[part, :].astype(F32)
        mu = jnp.mean(x, axis=1, keepdims=True)
        xc = x - mu
        r = lax.rsqrt(jnp.mean(xc * xc, axis=1, keepdims=True) + 1e-5)
        v = xc * r
        v_buf[part, :] = v
        r_buf[part, :] = jnp.broadcast_to(r, (CHUNK, 128))
        t = jnp.tanh(v * (C0 + (C0 * C1) * (v * v)))
        acts[part, :] = (v * (0.5 + 0.5 * t)).astype(BF16)

    w_copies[0].wait()
    h_send[0] = jnp.dot(acts[...], wt[0:channels, :], preferred_element_type=F32).astype(BF16)
    w_copies[1].wait()
    h_send[1] = jnp.dot(acts[...], wt[2 * channels:, :], preferred_element_type=F32).astype(BF16)
    pl.semaphore_wait(barrier, 15)

    h_up = remote(h_send.at[0], h_recv.at[0], hs_sem.at[0], hr_sem.at[0], jnp.minimum(me + 2, 15))
    h_down = remote(h_send.at[1], h_recv.at[1], hs_sem.at[1], hr_sem.at[1], jnp.maximum(me - 2, 0))

    @pl.when(me < 14)
    def _():
        h_up.start()

    @pl.when(me >= 2)
    def _():
        h_down.start()

    @pl.when(me < 2)
    def _():
        h_recv[0] = jnp.zeros(h_recv.shape[1:], BF16)

    @pl.when(me >= 14)
    def _():
        h_recv[1] = jnp.zeros(h_recv.shape[1:], BF16)

    acts_t[0:channels, :] = acts[...].astype(F32).T.astype(BF16)
    acts_t[channels:, :] = acts_t[0:own_rows, :]

    def block_of(target):
        return acts_t.at[pl.ds(pl.multiple_of((target * own_rows) % channels, SUB), own_rows)]

    a_copies = []
    for i in range(1, 8):
        peer = base + (place + i) % 8
        for b in range(2):
            copy = remote(block_of((peer + 8 * b) % 16), blocks.at[place, b],
                          as_sem.at[i, b], ar_sem.at[place, b], peer)
            copy.start()
            a_copies.append(copy)
    for b in range(2):
        blocks[place, b] = block_of((me + 8 * b) % 16)[...]

    dh[5 * half] = jnp.zeros(dh.shape[1:], BF16)

    w_copies[2].wait()
    h_mid = jnp.dot(acts[...], wt[channels:2 * channels, :], preferred_element_type=F32)
    w_copies[3].wait()
    back = nt_dot(ct_ref[...], wo[...])
    for n in range(rows // CHUNK):
        part = pl.ds(n * CHUNK, CHUNK)
        slope_buf[part, :] = gelu_pair(v_buf[part, :])[1]

    @pl.when(me >= 2)
    def _():
        h_up.wait_recv()

    @pl.when(me < 14)
    def _():
        h_down.wait_recv()

    hidden = h_mid + h_recv[0].astype(F32) + h_recv[1].astype(F32)
    gated, slope = gelu_pair(hidden)
    gated = gated.astype(BF16)
    mine = dh.at[1 + pair, pl.ds(pl.multiple_of(core * rows, rows), rows)]
    mine[...] = (back * slope).astype(BF16)

    spot = 2 * (1 + pair) + core
    d_copies = []
    for i in (2, 6, 1, 3, 7, 5, 4):
        peer = base + (place + i) % 8
        copy = remote(mine, mine, ds_sem.at[i], dr_sem.at[spot], peer)
        copy.start()
        d_copies.append(copy)

    edge_slot = 5 * half
    far = base + 8 - 16 * half
    at_edge = (me >= 6) & (me < 10)
    e_copies = [
        remote(mine, dh.at[edge_slot, pl.ds(pl.multiple_of(core * rows, rows), rows)],
               es_sem.at[i], dr_sem.at[2 * edge_slot + core], far + i)
        for i in range(8)
    ]

    @pl.when(at_edge)
    def _():
        for copy in e_copies:
            copy.start()

    out_ref[...] = (x_ref[...].astype(F32)
                    + jnp.dot(gated, wo[...], preferred_element_type=F32)).astype(BF16)

    def wait_slot(slot):
        remote(mine, mine, ds_sem.at[0], dr_sem.at[slot], mirror).wait_recv()

    lower, upper = spot - 2, spot + 2
    unused = 10 * half
    for slot in (lower, upper):
        @pl.when(slot // 2 != unused // 2)
        def _(slot=slot):
            wait_slot(slot)

    def core_rows(index):
        return dh[index, pl.ds(pl.multiple_of(core * rows, rows), rows), :]

    d_next, d_mid, d_prior = core_rows(pair + 2), core_rows(pair + 1), core_rows(pair)
    d_acts = nt_dot(d_next, wt[0:channels, :])
    d_acts = d_acts + nt_dot(d_mid, wt[channels:2 * channels, :])
    slope_buf[...] = (d_acts + nt_dot(d_prior, wt[2 * channels:, :])) * slope_buf[...]
    for n in range(rows // CHUNK):
        part = pl.ds(n * CHUNK, CHUNK)
        dv = slope_buf[part, :]
        v = v_buf[part, :]
        first = jnp.mean(dv, axis=1, keepdims=True)
        second = jnp.mean(dv * v, axis=1, keepdims=True)
        gi_ref[part, :] = (ct_ref[part, :].astype(F32)
                           + r_buf[part, 0:1] * (dv - first - v * second)).astype(BF16)

    for slot in range(12):
        @pl.when((slot != spot) & (slot != lower) & (slot != upper) & (slot // 2 != unused // 2))
        def _(slot=slot):
            wait_slot(slot)
    for i in range(1, 8):
        slot = (place + i) % 8
        for b in range(2):
            remote(blocks.at[slot, b], blocks.at[slot, b], as_sem.at[0, b],
                   ar_sem.at[slot, b], mirror).wait_recv()

    def term(b, j):
        tap = (3 * ((me + 8 * b) % 16) + j) // 16
        left = jnp.concatenate([blocks[s, b, j * SUB:(j + 1) * SUB, :] for s in range(8)], axis=1)
        right = dh[pl.ds(2 - tap, 4)].reshape(8 * rows, dh.shape[2])
        return jnp.dot(left, right, preferred_element_type=F32)

    for j in range(3):
        p_send[j * SUB:(j + 1) * SUB, :] = term(1, j).astype(BF16)
    p_copy = remote(p_send, p_recv, ps_sem, pr_sem, mirror)
    p_copy.start()
    for j in range(3):
        gt_ref[j * SUB:(j + 1) * SUB, :] = term(0, j)
    p_copy.wait_recv()
    gt_ref[...] = (gt_ref[...] + p_recv[...].astype(F32)) * scale

    @pl.when(me < 14)
    def _():
        h_up.wait_send()

    @pl.when(me >= 2)
    def _():
        h_down.wait_send()

    @pl.when(at_edge)
    def _():
        for copy in e_copies:
            copy.wait_send()

    for copy in a_copies + d_copies:
        copy.wait_send()
    p_copy.wait_send()


def fused_body(inputs, cotangent, w_taps, w_out):
    rows, channels = inputs.shape
    inner = w_taps.shape[1]
    count = lax.axis_size("ctx")
    own_rows = w_taps.shape[0] // count
    scale = 1.0 / math.sqrt(rows * count)
    vmem = pl.BlockSpec(memory_space=pltpu.VMEM)
    hbm = pl.BlockSpec(memory_space=pl.ANY)
    dma = pltpu.SemaphoreType.DMA
    return pl.pallas_call(
        functools.partial(fused, scale),
        out_shape=(
            jax.ShapeDtypeStruct((rows, channels), BF16),
            jax.ShapeDtypeStruct((rows, channels), BF16),
            jax.ShapeDtypeStruct((own_rows, inner), F32),
        ),
        in_specs=[vmem, vmem, hbm, hbm],
        out_specs=(vmem, vmem, vmem),
        scratch_shapes=[
            pltpu.VMEM(w_taps.shape, BF16),
            pltpu.VMEM(w_out.shape, BF16),
            pltpu.VMEM((rows, channels), BF16),
            pltpu.VMEM((channels + own_rows, rows), BF16),
            pltpu.VMEM((rows, channels), F32),
            pltpu.VMEM((rows, channels), F32),
            pltpu.VMEM((rows, 128), F32),
            pltpu.VMEM((8, 2, own_rows, rows), BF16),
            pltpu.VMEM((6, 2 * rows, inner), BF16),
            pltpu.VMEM((2, rows, inner), BF16),
            pltpu.VMEM((2, rows, inner), BF16),
            pltpu.VMEM((own_rows, inner), BF16),
            pltpu.VMEM((own_rows, inner), BF16),
            dma((4,)),
            dma((2,)),
            dma((2,)),
            dma((8, 2)),
            dma((8, 2)),
            dma((8,)),
            dma((12,)),
            dma((8,)),
            dma,
            dma,
        ],
        compiler_params=pltpu.CompilerParams(
            collective_id=0, has_side_effects=True, vmem_limit_bytes=48 * 1024 * 1024
        ),
    )(inputs, cotangent, w_taps, w_out)


def passed_along(array, axis, by):
    length = lax.axis_size(axis)
    pairs = [(i, i + by) for i in range(length) if 0 <= i + by < length]
    return lax.ppermute(array, axis, pairs)


def normalize(values):
    centre = jnp.mean(values, axis=1, keepdims=True)
    spread = jnp.mean(jnp.square(values - centre), axis=1, keepdims=True)
    return jax.nn.gelu((values - centre) * lax.rsqrt(spread + 1e-05))


def plain_body(inputs, cotangent, w_taps, w_out):
    hop = lax.axis_size("ctx") // 8
    rows, channels = inputs.shape
    scale = 1.0 / math.sqrt(rows * lax.axis_size("ctx"))
    w0, w1, w2 = (w_taps[k * channels:(k + 1) * channels] for k in range(3))
    as_float = inputs.astype(F32)
    acts_full, act_vjp = jax.vjp(normalize, as_float)
    acts = acts_full.astype(BF16)
    hidden = jnp.dot(acts, w1, preferred_element_type=F32)
    hidden += passed_along(jnp.dot(acts, w0, preferred_element_type=F32), "ctx", hop)
    hidden += passed_along(jnp.dot(acts, w2, preferred_element_type=F32), "ctx", -hop)
    gated_full, gelu_vjp = jax.vjp(jax.nn.gelu, hidden)
    outputs = (as_float + jnp.dot(gated_full.astype(BF16), w_out,
                                  preferred_element_type=F32)).astype(BF16)
    back = nt_dot(cotangent, w_out)
    dhid = gelu_vjp(back)[0].astype(BF16)
    d_next = passed_along(dhid, "ctx", -hop)
    d_prior = passed_along(dhid, "ctx", hop)
    terms = [
        lax.dot_general(acts, d, (((0,), (0,)), ((), ())), preferred_element_type=F32)
        for d in (d_next, dhid, d_prior)
    ]
    grad_taps = lax.psum_scatter(jnp.concatenate(terms, axis=0) * scale, "ctx",
                                 scatter_dimension=0, tiled=True)
    d_acts = nt_dot(d_next, w0) + nt_dot(dhid, w1) + nt_dot(d_prior, w2)
    grad_input = (cotangent.astype(F32) + act_vjp(d_acts)[0]).astype(BF16)
    return (outputs, grad_input, grad_taps)


def solution(mesh):
    spec = P(("groups", "ctx"), None)
    return jax.shard_map(
        fused_body if mesh.shape["ctx"] == 16 else plain_body,
        mesh=mesh,
        in_specs=(spec, spec, P(), P()),
        out_specs=(spec, spec, spec),
        check_vma=False,
    )
```

```python
import functools
import math

import jax
import jax.numpy as jnp
from jax import lax
from jax.experimental import pallas as pl
from jax.experimental.pallas import tpu as pltpu
from jax.sharding import PartitionSpec as P

F32 = jnp.float32
BF16 = jnp.bfloat16
C0 = math.sqrt(2.0 / math.pi)
C1 = 0.044715
CHUNK = 16
SUB = 96


def nt_dot(a, b):
    return lax.dot_general(a, b, (((1,), (1,)), ((), ())), preferred_element_type=F32)


def gelu_pair(v):
    sq = v * v
    t = jnp.tanh(v * (C0 + (C0 * C1) * sq))
    half = 0.5 + 0.5 * t
    value = v * half
    slope = half + (0.5 * v) * (1.0 - t * t) * (C0 + (3.0 * C0 * C1) * sq)
    return value, slope


def fused(
    scale, x_hbm, ct_hbm, wt_hbm, wo_hbm, out_ref, gi_ref, gt_ref,
    x_ref, ct_ref, wt, wo, acts, acts_t, v_buf, slope_buf, r_buf, blocks, dh, h_send, h_recv, p_send, p_recv,
    w_sem, hs_sem, hr_sem, as_sem, ar_sem, ds_sem, dr_sem, es_sem, fs_sem, ps_sem, pr_sem,
):
    me = lax.axis_index("ctx")
    rows, channels = x_ref.shape
    width = channels // 8
    half = me // 8
    base = half * 8
    place = me - base
    core = me % 2
    pair = place // 2
    mirror = (me + 8) % 16

    def to(index):
        return {"ctx": index}

    def remote(src, dst, send, recv, index):
        return pltpu.make_async_remote_copy(
            src_ref=src, dst_ref=dst, send_sem=send, recv_sem=recv,
            device_id=to(index), device_id_type=pl.DeviceIdType.MESH,
        )

    w_copies = [
        pltpu.make_async_copy(wt_hbm.at[pl.ds(k * channels, channels)],
                              wt.at[pl.ds(k * channels, channels)], w_sem.at[n])
        for n, k in enumerate((0, 2, 1))
    ]
    w_copies.append(pltpu.make_async_copy(wo_hbm, wo, w_sem.at[3]))
    x_copy = pltpu.make_async_copy(x_hbm, x_ref, w_sem.at[4])
    ct_copy = pltpu.make_async_copy(ct_hbm, ct_ref, w_sem.at[5])
    for copy in (x_copy, *w_copies, ct_copy):
        copy.start()

    barrier = pltpu.get_barrier_semaphore()
    for i in range(1, 16):
        pl.semaphore_signal(barrier, inc=1, device_id=to((me + i) % 16),
                            device_id_type=pl.DeviceIdType.MESH)

    x_copy.wait()
    for n in range(rows // CHUNK):
        part = pl.ds(n * CHUNK, CHUNK)
        x = x_ref[part, :].astype(F32)
        mu = jnp.mean(x, axis=1, keepdims=True)
        xc = x - mu
        r = lax.rsqrt(jnp.mean(xc * xc, axis=1, keepdims=True) + 1e-5)
        v = xc * r
        v_buf[part, :] = v
        r_buf[part, :] = jnp.broadcast_to(r, (CHUNK, 128))
        t = jnp.tanh(v * (C0 + (C0 * C1) * (v * v)))
        acts[part, :] = (v * (0.5 + 0.5 * t)).astype(BF16)

    w_copies[0].wait()
    h_send[0] = jnp.dot(acts[...], wt[0:channels, :], preferred_element_type=F32).astype(BF16)
    w_copies[1].wait()
    h_send[1] = jnp.dot(acts[...], wt[2 * channels:, :], preferred_element_type=F32).astype(BF16)
    pl.semaphore_wait(barrier, 15)

    h_up = remote(h_send.at[0], h_recv.at[0], hs_sem.at[0], hr_sem.at[0], jnp.minimum(me + 2, 15))
    h_down = remote(h_send.at[1], h_recv.at[1], hs_sem.at[1], hr_sem.at[1], jnp.maximum(me - 2, 0))

    @pl.when(me < 14)
    def _():
        h_up.start()

    @pl.when(me >= 2)
    def _():
        h_down.start()

    @pl.when(me < 2)
    def _():
        h_recv[0] = jnp.zeros(h_recv.shape[1:], BF16)

    @pl.when(me >= 14)
    def _():
        h_recv[1] = jnp.zeros(h_recv.shape[1:], BF16)

    acts_t[...] = acts[...].astype(F32).T.astype(BF16)

    def block_of(spot):
        return acts_t.at[pl.ds(pl.multiple_of(spot * width, width), width)]

    a_copies = []
    for i in range(1, 8):
        peer = (place + i) % 8
        copy = remote(block_of(peer), blocks.at[place], as_sem.at[i], ar_sem.at[place], base + peer)
        copy.start()
        a_copies.append(copy)
    blocks[place] = block_of(place)[...]

    dh[5 * half] = jnp.zeros(dh.shape[1:], BF16)

    w_copies[2].wait()
    h_mid = jnp.dot(acts[...], wt[channels:2 * channels, :], preferred_element_type=F32)
    w_copies[3].wait()
    ct_copy.wait()
    back = nt_dot(ct_ref[...], wo[...])
    for n in range(rows // CHUNK):
        part = pl.ds(n * CHUNK, CHUNK)
        slope_buf[part, :] = gelu_pair(v_buf[part, :])[1]

    @pl.when(me >= 2)
    def _():
        h_up.wait_recv()

    @pl.when(me < 14)
    def _():
        h_down.wait_recv()

    hidden = h_mid + h_recv[0].astype(F32) + h_recv[1].astype(F32)
    gated, slope = gelu_pair(hidden)
    gated = gated.astype(BF16)
    mine = dh.at[1 + pair, pl.ds(pl.multiple_of(core * rows, rows), rows)]
    mine[...] = (back * slope).astype(BF16)

    spot = 2 * (1 + pair) + core
    sibling = me + 1 - 2 * core
    core_part = pl.ds(pl.multiple_of(core * rows, rows), rows)
    edge_index = 5 * half
    far = base + 8 - 16 * half
    d_copies = []
    for i in (1, 3, 2):
        peer = base + 2 * ((pair + i) % 4) + core
        d_copies.append(remote(mine, mine, ds_sem.at[i], dr_sem.at[spot], peer))
    d_copies.append(remote(mine, mine, ds_sem.at[0], dr_sem.at[spot], sibling))
    at_edge = (me >= 6) & (me < 10)
    e_copies = [
        remote(mine, dh.at[edge_index, core_part], es_sem.at[i],
               dr_sem.at[2 * edge_index + core], far + 2 * i + core)
        for i in range(4)
    ]
    for copy in d_copies[:2]:
        copy.start()

    @pl.when(at_edge)
    def _():
        for copy in e_copies:
            copy.start()

    for copy in d_copies[2:]:
        copy.start()

    out_ref[...] = (x_ref[...].astype(F32)
                    + jnp.dot(gated, wo[...], preferred_element_type=F32)).astype(BF16)

    def wait_slot(slot):
        remote(mine, mine, ds_sem.at[0], dr_sem.at[slot], mirror).wait_recv()

    outer = 5 - edge_index
    f_copies = []
    for i, index in enumerate((1 + (pair + 1) % 4, 1 + (pair + 3) % 4, outer, 1 + (pair + 2) % 4)):
        slot = dh.at[index, core_part]
        wait_slot(2 * index + core)
        copy = remote(slot, slot, fs_sem.at[i], dr_sem.at[2 * index + core], sibling)
        copy.start()
        f_copies.append(copy)

    def core_rows(index):
        return dh[index, pl.ds(pl.multiple_of(core * rows, rows), rows), :]

    d_next, d_mid, d_prior = core_rows(pair + 2), core_rows(pair + 1), core_rows(pair)
    d_acts = nt_dot(d_next, wt[0:channels, :])
    d_acts = d_acts + nt_dot(d_mid, wt[channels:2 * channels, :])
    slope_buf[...] = (d_acts + nt_dot(d_prior, wt[2 * channels:, :])) * slope_buf[...]
    for n in range(rows // CHUNK):
        part = pl.ds(n * CHUNK, CHUNK)
        dv = slope_buf[part, :]
        v = v_buf[part, :]
        first = jnp.mean(dv, axis=1, keepdims=True)
        second = jnp.mean(dv * v, axis=1, keepdims=True)
        gi_ref[part, :] = (ct_ref[part, :].astype(F32)
                           + r_buf[part, 0:1] * (dv - first - v * second)).astype(BF16)

    for i in range(1, 8):
        slot = (place + i) % 8
        remote(blocks.at[slot], blocks.at[slot], as_sem.at[0], ar_sem.at[slot], mirror).wait_recv()
    for i in range(4):
        wait_slot(2 * (1 + (pair + i) % 4) + 1 - core)
    wait_slot(2 * outer + 1 - core)

    left = jnp.concatenate([blocks[i] for i in range(8)], axis=1)
    p_copies = []
    for n in range(3):
        tap = (1 - half) * (2 - n) + half * n
        right = dh[pl.ds(2 - tap, 4)].reshape(8 * rows, dh.shape[2])
        term = jnp.dot(left, right, preferred_element_type=F32).astype(BF16)
        for u in range(2):
            piece = 16 * tap + 2 * place + u
            owner = piece // 3
            spare = p_send.at[2 * n + u]
            spare[...] = term[u * SUB:(u + 1) * SUB, :]
            copy = remote(spare, p_recv.at[half, piece % 3], ps_sem.at[2 * n + u],
                          pr_sem.at[half, piece % 3], owner)
            p_copies.append((owner, copy))

            @pl.when(owner != me)
            def _(copy=copy):
                copy.start()

            @pl.when(owner == me)
            def _(spare=spare, piece=piece):
                p_recv[half, piece % 3] = spare[...]

    for j in range(3):
        for h in range(2):
            maker = 8 * h + ((3 * me + j) % 16) // 2

            @pl.when(maker != me)
            def _(h=h, j=j):
                remote(p_send.at[0], p_recv.at[h, j], ps_sem.at[0], pr_sem.at[h, j],
                       mirror).wait_recv()

        gt_ref[j * SUB:(j + 1) * SUB, :] = (
            p_recv[0, j].astype(F32) + p_recv[1, j].astype(F32)) * scale

    @pl.when(me < 14)
    def _():
        h_up.wait_send()

    @pl.when(me >= 2)
    def _():
        h_down.wait_send()

    @pl.when(at_edge)
    def _():
        for copy in e_copies:
            copy.wait_send()

    for copy in a_copies + d_copies + f_copies:
        copy.wait_send()
    for owner, copy in p_copies:
        @pl.when(owner != me)
        def _(copy=copy):
            copy.wait_send()


def fused_body(inputs, cotangent, w_taps, w_out):
    rows, channels = inputs.shape
    inner = w_taps.shape[1]
    count = lax.axis_size("ctx")
    own_rows = w_taps.shape[0] // count
    scale = 1.0 / math.sqrt(rows * count)
    vmem = pl.BlockSpec(memory_space=pltpu.VMEM)
    hbm = pl.BlockSpec(memory_space=pl.ANY)
    dma = pltpu.SemaphoreType.DMA
    return pl.pallas_call(
        functools.partial(fused, scale),
        out_shape=(
            jax.ShapeDtypeStruct((rows, channels), BF16),
            jax.ShapeDtypeStruct((rows, channels), BF16),
            jax.ShapeDtypeStruct((own_rows, inner), F32),
        ),
        in_specs=[hbm, hbm, hbm, hbm],
        out_specs=(vmem, vmem, vmem),
        scratch_shapes=[
            pltpu.VMEM((rows, channels), BF16),
            pltpu.VMEM((rows, channels), BF16),
            pltpu.VMEM(w_taps.shape, BF16),
            pltpu.VMEM(w_out.shape, BF16),
            pltpu.VMEM((rows, channels), BF16),
            pltpu.VMEM((channels, rows), BF16),
            pltpu.VMEM((rows, channels), F32),
            pltpu.VMEM((rows, channels), F32),
            pltpu.VMEM((rows, 128), F32),
            pltpu.VMEM((8, channels // 8, rows), BF16),
            pltpu.VMEM((6, 2 * rows, inner), BF16),
            pltpu.VMEM((2, rows, inner), BF16),
            pltpu.VMEM((2, rows, inner), BF16),
            pltpu.VMEM((6, SUB, inner), BF16),
            pltpu.VMEM((2, 3, SUB, inner), BF16),
            dma((6,)),
            dma((2,)),
            dma((2,)),
            dma((8,)),
            dma((8,)),
            dma((4,)),
            dma((12,)),
            dma((4,)),
            dma((4,)),
            dma((6,)),
            dma((2, 3)),
        ],
        compiler_params=pltpu.CompilerParams(
            collective_id=0, has_side_effects=True, vmem_limit_bytes=60 * 1024 * 1024
        ),
    )(inputs, cotangent, w_taps, w_out)


def passed_along(array, axis, by):
    length = lax.axis_size(axis)
    pairs = [(i, i + by) for i in range(length) if 0 <= i + by < length]
    return lax.ppermute(array, axis, pairs)


def normalize(values):
    centre = jnp.mean(values, axis=1, keepdims=True)
    spread = jnp.mean(jnp.square(values - centre), axis=1, keepdims=True)
    return jax.nn.gelu((values - centre) * lax.rsqrt(spread + 1e-05))


def plain_body(inputs, cotangent, w_taps, w_out):
    hop = lax.axis_size("ctx") // 8
    rows, channels = inputs.shape
    scale = 1.0 / math.sqrt(rows * lax.axis_size("ctx"))
    w0, w1, w2 = (w_taps[k * channels:(k + 1) * channels] for k in range(3))
    as_float = inputs.astype(F32)
    acts_full, act_vjp = jax.vjp(normalize, as_float)
    acts = acts_full.astype(BF16)
    hidden = jnp.dot(acts, w1, preferred_element_type=F32)
    hidden += passed_along(jnp.dot(acts, w0, preferred_element_type=F32), "ctx", hop)
    hidden += passed_along(jnp.dot(acts, w2, preferred_element_type=F32), "ctx", -hop)
    gated_full, gelu_vjp = jax.vjp(jax.nn.gelu, hidden)
    outputs = (as_float + jnp.dot(gated_full.astype(BF16), w_out,
                                  preferred_element_type=F32)).astype(BF16)
    back = nt_dot(cotangent, w_out)
    dhid = gelu_vjp(back)[0].astype(BF16)
    d_next = passed_along(dhid, "ctx", -hop)
    d_prior = passed_along(dhid, "ctx", hop)
    terms = [
        lax.dot_general(acts, d, (((0,), (0,)), ((), ())), preferred_element_type=F32)
        for d in (d_next, dhid, d_prior)
    ]
    grad_taps = lax.psum_scatter(jnp.concatenate(terms, axis=0) * scale, "ctx",
                                 scatter_dimension=0, tiled=True)
    d_acts = nt_dot(d_next, w0) + nt_dot(dhid, w1) + nt_dot(d_prior, w2)
    grad_input = (cotangent.astype(F32) + act_vjp(d_acts)[0]).astype(BF16)
    return (outputs, grad_input, grad_taps)


def solution(mesh):
    spec = P(("groups", "ctx"), None)
    return jax.shard_map(
        fused_body if mesh.shape["ctx"] == 16 else plain_body,
        mesh=mesh,
        in_specs=(spec, spec, P(), P()),
        out_specs=(spec, spec, spec),
        check_vma=False,
    )
```

```python
import functools
import math

import jax
import jax.numpy as jnp
from jax import lax
from jax.experimental import pallas as pl
from jax.experimental.pallas import tpu as pltpu
from jax.sharding import PartitionSpec as P

F32 = jnp.float32
BF16 = jnp.bfloat16
C0 = math.sqrt(2.0 / math.pi)
C1 = 0.044715
CHUNK = 16
SUB = 96


def nt_dot(a, b):
    return lax.dot_general(a, b, (((1,), (1,)), ((), ())), preferred_element_type=F32)


def gelu_pair(v):
    sq = v * v
    t = jnp.tanh(v * (C0 + (C0 * C1) * sq))
    half = 0.5 + 0.5 * t
    value = v * half
    slope = half + (0.5 * v) * (1.0 - t * t) * (C0 + (3.0 * C0 * C1) * sq)
    return value, slope


def fused(
    scale, x_hbm, ct_hbm, wt_hbm, wo_hbm, out_ref, gi_ref, gt_ref,
    x_ref, ct_ref, wt, wo, acts, acts_t, v_buf, slope_buf, r_buf, blocks, dh, h_send, h_recv, p_send, p_recv,
    w_sem, hs_sem, hr_sem, as_sem, ar_sem, ds_sem, dr_sem, es_sem, fs_sem, ps_sem, pr_sem,
):
    me = lax.axis_index("ctx")
    rows, channels = x_ref.shape
    width = channels // 8
    half = me // 8
    base = half * 8
    place = me - base
    core = me % 2
    pair = place // 2
    mirror = (me + 8) % 16

    def to(index):
        return {"ctx": index}

    def remote(src, dst, send, recv, index):
        return pltpu.make_async_remote_copy(
            src_ref=src, dst_ref=dst, send_sem=send, recv_sem=recv,
            device_id=to(index), device_id_type=pl.DeviceIdType.MESH,
        )

    w_copies = [
        pltpu.make_async_copy(wt_hbm.at[pl.ds(k * channels, channels)],
                              wt.at[pl.ds(k * channels, channels)], w_sem.at[n])
        for n, k in enumerate((0, 2, 1))
    ]
    w_copies.append(pltpu.make_async_copy(wo_hbm, wo, w_sem.at[3]))
    x_copy = pltpu.make_async_copy(x_hbm, x_ref, w_sem.at[4])
    ct_copy = pltpu.make_async_copy(ct_hbm, ct_ref, w_sem.at[5])
    for copy in (x_copy, *w_copies, ct_copy):
        copy.start()

    barrier = pltpu.get_barrier_semaphore()
    for i in range(1, 16):
        pl.semaphore_signal(barrier, inc=1, device_id=to((me + i) % 16),
                            device_id_type=pl.DeviceIdType.MESH)

    x_copy.wait()
    for n in range(rows // CHUNK):
        part = pl.ds(n * CHUNK, CHUNK)
        x = x_ref[part, :].astype(F32)
        mu = jnp.mean(x, axis=1, keepdims=True)
        xc = x - mu
        r = lax.rsqrt(jnp.mean(xc * xc, axis=1, keepdims=True) + 1e-5)
        v = xc * r
        v_buf[part, :] = v
        r_buf[part, :] = jnp.broadcast_to(r, (CHUNK, 128))
        t = jnp.tanh(v * (C0 + (C0 * C1) * (v * v)))
        acts[part, :] = (v * (0.5 + 0.5 * t)).astype(BF16)

    w_copies[0].wait()
    h_send[0] = jnp.dot(acts[...], wt[0:channels, :], preferred_element_type=F32).astype(BF16)
    w_copies[1].wait()
    h_send[1] = jnp.dot(acts[...], wt[2 * channels:, :], preferred_element_type=F32).astype(BF16)
    pl.semaphore_wait(barrier, 15)

    h_up = remote(h_send.at[0], h_recv.at[0], hs_sem.at[0], hr_sem.at[0], jnp.minimum(me + 2, 15))
    h_down = remote(h_send.at[1], h_recv.at[1], hs_sem.at[1], hr_sem.at[1], jnp.maximum(me - 2, 0))

    @pl.when(me < 14)
    def _():
        h_up.start()

    @pl.when(me >= 2)
    def _():
        h_down.start()

    @pl.when(me < 2)
    def _():
        h_recv[0] = jnp.zeros(h_recv.shape[1:], BF16)

    @pl.when(me >= 14)
    def _():
        h_recv[1] = jnp.zeros(h_recv.shape[1:], BF16)

    acts_t[...] = acts[...].astype(F32).T.astype(BF16)

    def block_of(spot):
        return acts_t.at[pl.ds(pl.multiple_of(spot * width, width), width)]

    a_copies = []
    for i in range(1, 8):
        peer = (place + i) % 8
        copy = remote(block_of(peer), blocks.at[place], as_sem.at[i], ar_sem.at[place], base + peer)
        copy.start()
        a_copies.append(copy)
    blocks[place] = block_of(place)[...]

    dh[5 * half] = jnp.zeros(dh.shape[1:], BF16)

    w_copies[2].wait()
    h_mid = jnp.dot(acts[...], wt[channels:2 * channels, :], preferred_element_type=F32)
    w_copies[3].wait()
    ct_copy.wait()
    back = nt_dot(ct_ref[...], wo[...])
    for n in range(rows // CHUNK):
        part = pl.ds(n * CHUNK, CHUNK)
        slope_buf[part, :] = gelu_pair(v_buf[part, :])[1]

    @pl.when(me >= 2)
    def _():
        h_up.wait_recv()

    @pl.when(me < 14)
    def _():
        h_down.wait_recv()

    hidden = h_mid + h_recv[0].astype(F32) + h_recv[1].astype(F32)
    gated, slope = gelu_pair(hidden)
    gated = gated.astype(BF16)
    mine = dh.at[1 + pair, pl.ds(pl.multiple_of(core * rows, rows), rows)]
    mine[...] = (back * slope).astype(BF16)

    spot = 2 * (1 + pair) + core
    sibling = me + 1 - 2 * core
    core_part = pl.ds(pl.multiple_of(core * rows, rows), rows)
    edge_index = 5 * half
    far = base + 8 - 16 * half
    d_copies = []
    for i in (1, 3, 2):
        peer = base + 2 * ((pair + i) % 4) + core
        d_copies.append(remote(mine, mine, ds_sem.at[i], dr_sem.at[spot], peer))
    d_copies.append(remote(mine, mine, ds_sem.at[0], dr_sem.at[spot], sibling))
    at_edge = (me >= 6) & (me < 10)
    e_copies = [
        remote(mine, dh.at[edge_index, core_part], es_sem.at[i],
               dr_sem.at[2 * edge_index + core], far + 2 * i + core)
        for i in range(4)
    ]
    for copy in d_copies[:2]:
        copy.start()

    @pl.when(at_edge)
    def _():
        for copy in e_copies:
            copy.start()

    for copy in d_copies[2:]:
        copy.start()

    def wait_slot(slot):
        remote(mine, mine, ds_sem.at[0], dr_sem.at[slot], mirror).wait_recv()

    outer = 5 - edge_index
    f_copies = []
    for i, index in enumerate((1 + (pair + 1) % 4, 1 + (pair + 3) % 4, outer, 1 + (pair + 2) % 4)):
        slot = dh.at[index, core_part]
        wait_slot(2 * index + core)
        copy = remote(slot, slot, fs_sem.at[i], dr_sem.at[2 * index + core], sibling)
        copy.start()
        f_copies.append(copy)

    for i in range(1, 8):
        slot = (place + i) % 8
        remote(blocks.at[slot], blocks.at[slot], as_sem.at[0], ar_sem.at[slot], mirror).wait_recv()
    for i in range(4):
        wait_slot(2 * (1 + (pair + i) % 4) + 1 - core)
    wait_slot(2 * outer + 1 - core)

    left = jnp.concatenate([blocks[i] for i in range(8)], axis=1)
    p_copies = []
    for n in range(3):
        tap = (1 - half) * (2 - n) + half * n
        right = dh[pl.ds(2 - tap, 4)].reshape(8 * rows, dh.shape[2])
        term = jnp.dot(left, right, preferred_element_type=F32).astype(BF16)
        for u in range(2):
            piece = 16 * tap + 2 * place + u
            owner = piece // 3
            spare = p_send.at[2 * n + u]
            spare[...] = term[u * SUB:(u + 1) * SUB, :]
            copy = remote(spare, p_recv.at[half, piece % 3], ps_sem.at[2 * n + u],
                          pr_sem.at[half, piece % 3], owner)
            p_copies.append((owner, copy))

            @pl.when(owner != me)
            def _(copy=copy):
                copy.start()

            @pl.when(owner == me)
            def _(spare=spare, piece=piece):
                p_recv[half, piece % 3] = spare[...]

    out_ref[...] = (x_ref[...].astype(F32)
                    + jnp.dot(gated, wo[...], preferred_element_type=F32)).astype(BF16)

    def core_rows(index):
        return dh[index, pl.ds(pl.multiple_of(core * rows, rows), rows), :]

    d_next, d_mid, d_prior = core_rows(pair + 2), core_rows(pair + 1), core_rows(pair)
    d_acts = nt_dot(d_next, wt[0:channels, :])
    d_acts = d_acts + nt_dot(d_mid, wt[channels:2 * channels, :])
    slope_buf[...] = (d_acts + nt_dot(d_prior, wt[2 * channels:, :])) * slope_buf[...]
    for n in range(rows // CHUNK):
        part = pl.ds(n * CHUNK, CHUNK)
        dv = slope_buf[part, :]
        v = v_buf[part, :]
        first = jnp.mean(dv, axis=1, keepdims=True)
        second = jnp.mean(dv * v, axis=1, keepdims=True)
        gi_ref[part, :] = (ct_ref[part, :].astype(F32)
                           + r_buf[part, 0:1] * (dv - first - v * second)).astype(BF16)

    for j in range(3):
        for h in range(2):
            maker = 8 * h + ((3 * me + j) % 16) // 2

            @pl.when(maker != me)
            def _(h=h, j=j):
                remote(p_send.at[0], p_recv.at[h, j], ps_sem.at[0], pr_sem.at[h, j],
                       mirror).wait_recv()

        gt_ref[j * SUB:(j + 1) * SUB, :] = (
            p_recv[0, j].astype(F32) + p_recv[1, j].astype(F32)) * scale

    @pl.when(me < 14)
    def _():
        h_up.wait_send()

    @pl.when(me >= 2)
    def _():
        h_down.wait_send()

    @pl.when(at_edge)
    def _():
        for copy in e_copies:
            copy.wait_send()

    for copy in a_copies + d_copies + f_copies:
        copy.wait_send()
    for owner, copy in p_copies:
        @pl.when(owner != me)
        def _(copy=copy):
            copy.wait_send()


def fused_body(inputs, cotangent, w_taps, w_out):
    rows, channels = inputs.shape
    inner = w_taps.shape[1]
    count = lax.axis_size("ctx")
    own_rows = w_taps.shape[0] // count
    scale = 1.0 / math.sqrt(rows * count)
    vmem = pl.BlockSpec(memory_space=pltpu.VMEM)
    hbm = pl.BlockSpec(memory_space=pl.ANY)
    dma = pltpu.SemaphoreType.DMA
    return pl.pallas_call(
        functools.partial(fused, scale),
        out_shape=(
            jax.ShapeDtypeStruct((rows, channels), BF16),
            jax.ShapeDtypeStruct((rows, channels), BF16),
            jax.ShapeDtypeStruct((own_rows, inner), F32),
        ),
        in_specs=[hbm, hbm, hbm, hbm],
        out_specs=(vmem, vmem, vmem),
        scratch_shapes=[
            pltpu.VMEM((rows, channels), BF16),
            pltpu.VMEM((rows, channels), BF16),
            pltpu.VMEM(w_taps.shape, BF16),
            pltpu.VMEM(w_out.shape, BF16),
            pltpu.VMEM((rows, channels), BF16),
            pltpu.VMEM((channels, rows), BF16),
            pltpu.VMEM((rows, channels), F32),
            pltpu.VMEM((rows, channels), F32),
            pltpu.VMEM((rows, 128), F32),
            pltpu.VMEM((8, channels // 8, rows), BF16),
            pltpu.VMEM((6, 2 * rows, inner), BF16),
            pltpu.VMEM((2, rows, inner), BF16),
            pltpu.VMEM((2, rows, inner), BF16),
            pltpu.VMEM((6, SUB, inner), BF16),
            pltpu.VMEM((2, 3, SUB, inner), BF16),
            dma((6,)),
            dma((2,)),
            dma((2,)),
            dma((8,)),
            dma((8,)),
            dma((4,)),
            dma((12,)),
            dma((4,)),
            dma((4,)),
            dma((6,)),
            dma((2, 3)),
        ],
        compiler_params=pltpu.CompilerParams(
            collective_id=0, has_side_effects=True, vmem_limit_bytes=60 * 1024 * 1024
        ),
    )(inputs, cotangent, w_taps, w_out)


def passed_along(array, axis, by):
    length = lax.axis_size(axis)
    pairs = [(i, i + by) for i in range(length) if 0 <= i + by < length]
    return lax.ppermute(array, axis, pairs)


def normalize(values):
    centre = jnp.mean(values, axis=1, keepdims=True)
    spread = jnp.mean(jnp.square(values - centre), axis=1, keepdims=True)
    return jax.nn.gelu((values - centre) * lax.rsqrt(spread + 1e-05))


def plain_body(inputs, cotangent, w_taps, w_out):
    hop = lax.axis_size("ctx") // 8
    rows, channels = inputs.shape
    scale = 1.0 / math.sqrt(rows * lax.axis_size("ctx"))
    w0, w1, w2 = (w_taps[k * channels:(k + 1) * channels] for k in range(3))
    as_float = inputs.astype(F32)
    acts_full, act_vjp = jax.vjp(normalize, as_float)
    acts = acts_full.astype(BF16)
    hidden = jnp.dot(acts, w1, preferred_element_type=F32)
    hidden += passed_along(jnp.dot(acts, w0, preferred_element_type=F32), "ctx", hop)
    hidden += passed_along(jnp.dot(acts, w2, preferred_element_type=F32), "ctx", -hop)
    gated_full, gelu_vjp = jax.vjp(jax.nn.gelu, hidden)
    outputs = (as_float + jnp.dot(gated_full.astype(BF16), w_out,
                                  preferred_element_type=F32)).astype(BF16)
    back = nt_dot(cotangent, w_out)
    dhid = gelu_vjp(back)[0].astype(BF16)
    d_next = passed_along(dhid, "ctx", -hop)
    d_prior = passed_along(dhid, "ctx", hop)
    terms = [
        lax.dot_general(acts, d, (((0,), (0,)), ((), ())), preferred_element_type=F32)
        for d in (d_next, dhid, d_prior)
    ]
    grad_taps = lax.psum_scatter(jnp.concatenate(terms, axis=0) * scale, "ctx",
                                 scatter_dimension=0, tiled=True)
    d_acts = nt_dot(d_next, w0) + nt_dot(dhid, w1) + nt_dot(d_prior, w2)
    grad_input = (cotangent.astype(F32) + act_vjp(d_acts)[0]).astype(BF16)
    return (outputs, grad_input, grad_taps)


def solution(mesh):
    spec = P(("groups", "ctx"), None)
    return jax.shard_map(
        fused_body if mesh.shape["ctx"] == 16 else plain_body,
        mesh=mesh,
        in_specs=(spec, spec, P(), P()),
        out_specs=(spec, spec, spec),
        check_vma=False,
    )
```
